32 devices in a mesh: dom: 8 (over y, x, core), band: 4 (over z).
Axes of the slice: x: 2, y: 2, z: 4, core: 2. Of those that a mesh axis runs over, the one named last changes fastest.
Arguments:
- waves: float32 [2048, 2048], P('dom', 'band'), may hold values from -6 to 6
- cell_matrix: float32 [64, 125, 125], P('dom')
- connect: int32 [64, 125], P('dom'), may hold values from 0 to 383, as said below
- send_index: int32 [8, 2, 64], P('dom'), may hold values from 0 to 255
- rotation: float32 [2048, 2048], P('band'), may hold values from -0.125 to 0.125
Outputs:
- rotated: float32 [2048, 2048], P('dom', 'band')
The draws below stay inside these ranges and needn't reach their ends.
Inputs may be any that keep to these rules, and one draw needn't show every extreme that they name: On domain d, an entry of connect at or above 256 is 256 + k * 64 + s where s is below the number of slots that domain (d - 1 + 2 k) mod 8 fills on face k: exactly 64 for k = 1, between 64 // 2 (at least 1) and 64, uneven over domains, for k = 0; only those slots of send_index matter.
All inputs are finite; a program needn't handle non-finite values.
Results may differ from the reference program's by a relative error of at most 0.00012.
Values sent between devices are 32-bit elements; how exact they have to be, the bound alone decides.
A program may use at most 64 MiB of HBM per device.

```python
import jax
import jax.numpy as jnp
from jax import lax

BANDS = 2048
NPC = 125
DEGREE = 8
NOWN = 256
SLOT = 64
CELLS = 8
N_NODES = 2048
N_DOM = 8


def slot_counts(key):
    count_key = jax.random.fold_in(key, 7)
    lowest = max(1, SLOT // 2)
    uneven = jax.random.randint(count_key, (N_DOM,), lowest, SLOT + 1)
    full = jnp.full((N_DOM,), SLOT, jnp.int32)
    return jnp.stack([uneven.astype(jnp.int32), full], axis=1).astype(jnp.int32)


def draw_connect(key, part):
    counts = slot_counts(key)
    row_total = N_DOM * CELLS
    first, second, third, fourth = jax.random.split(jax.random.fold_in(key, 11), 4)
    device = (jnp.arange(row_total, dtype=jnp.int32) // CELLS)[:, None]
    device = jnp.broadcast_to(device, (row_total, NPC))
    ghost_pick = jax.random.randint(first, (row_total, NPC), 0, 4) == 0
    owned = jax.random.randint(second, (row_total, NPC), 0, NOWN)
    side = jax.random.randint(third, (row_total, NPC), 0, 2)
    source = (device - 1 + 2 * side) % N_DOM
    limit = counts[source, side]
    slot_pos = jax.random.randint(fourth, (row_total, NPC), 0, 1 << 20) % limit
    ghost = NOWN + side * SLOT + slot_pos
    result = jnp.where(ghost_pick, ghost, owned)
    cell_pos = jnp.arange(row_total, dtype=jnp.int32)[:, None] % CELLS
    column = jnp.arange(NPC, dtype=jnp.int32)[None, :]
    forced = NOWN + 2 * SLOT - 1
    result = jnp.where((cell_pos == 0) & (column == 0), forced, result)
    result = jnp.where((cell_pos == 0) & (column == 1), 0, result)
    return result.astype(jnp.int32)


def draw_cell_matrix(key, part):
    row_total = N_DOM * CELLS
    first, second = jax.random.split(jax.random.fold_in(key, 23), 2)
    raw = jax.random.normal(first, (row_total, NPC, NPC), jnp.float32)
    raw = raw * (0.6 / NPC ** 0.5)
    symmetric = (raw + jnp.swapaxes(raw, 1, 2)) * 0.70710678
    diagonal = jax.random.uniform(second, (row_total, NPC), jnp.float32, 0.5, 1.5)
    on_diag = jnp.arange(NPC)[:, None] == jnp.arange(NPC)[None, :]
    return jnp.where(on_diag[None, :, :], diagonal[:, :, None], symmetric).astype(jnp.float32)


def touch_ends(values, rng, smallest, largest):
    longest = values.shape.index(max(values.shape))
    spots = []
    for shift in (0, 1):
        where = [jax.random.randint(jax.random.fold_in(rng, axis), (), 0, length) for axis, length in enumerate(values.shape)]
        where[longest] = (where[longest] + shift) % values.shape[longest]
        spots.append(tuple(where))
    return values.at[spots[0]].set(smallest).at[spots[1]].set(largest)


def level_of(own_key, shape, pieces, least, high):
    level, own = 1.0, jax.random.fold_in(own_key, 6)
    for axis_at, parts in pieces:
        draws = jnp.exp(jax.random.uniform(jax.random.fold_in(own, axis_at), (parts,), jnp.float32, least / len(pieces), high / len(pieces)))
        level = level * jnp.repeat(draws, shape[axis_at] // parts).reshape([-1 if axis == axis_at else 1 for axis in range(len(shape))])
    return level


def noise(own_key, shape, spread, most, pieces=(), held_as=jnp.bfloat16):
    values = spread * jax.random.normal(own_key, shape, jnp.float32)
    if pieces:
        values = values * level_of(own_key, shape, pieces, -0.22, 0.18)
    return jnp.clip(values, -most, most).astype(held_as)


def setup_inputs(seed: int = 0) -> dict:
    seeds = jax.random.split(jax.random.key(seed), 6)
    waves = noise(seeds[0], (N_NODES, BANDS), 1.0, 6.0, ((0, 8), (1, 4)), jnp.float32)
    cell_matrix = draw_cell_matrix(jax.random.fold_in(seeds[5], 71), 0)
    connect = draw_connect(jax.random.fold_in(seeds[5], 71), 0)
    send_index = touch_ends(jax.random.randint(seeds[3], (N_DOM, 2, SLOT), 0, NOWN), jax.random.fold_in(seeds[3], 1), 0, NOWN - 1).astype(jnp.int32)
    rotation = noise(seeds[4], (BANDS, BANDS), BANDS ** -0.5, 0.125, ((0, 4),), jnp.float32)
    return dict(waves=waves, cell_matrix=cell_matrix, connect=connect, send_index=send_index, rotation=rotation)


centre = 5.5
half_width = 9.5


def assemble_ids(connect, send_index):
    device = (jnp.arange(connect.shape[0], dtype=jnp.int32) // CELLS)[:, None]
    device = jnp.broadcast_to(device, connect.shape).astype(jnp.int32)
    shifted = connect - NOWN
    is_ghost = shifted >= 0
    shifted = jnp.where(is_ghost, shifted, 0).astype(jnp.int32)
    side = (shifted // SLOT).astype(jnp.int32)
    slot_pos = (shifted % SLOT).astype(jnp.int32)
    source = ((device - 1 + 2 * side) % N_DOM).astype(jnp.int32)
    remote = source * NOWN + send_index[source, side, slot_pos]
    local = device * NOWN + connect
    return jnp.where(is_ghost, remote, local).astype(jnp.int32)


def operator_apply(vector, cell_matrix, global_ids):
    matrices = cell_matrix.reshape(N_DOM, CELLS, NPC, NPC)
    node_ids = global_ids.reshape(N_DOM, CELLS, NPC)

    def one_block(running, inputs):
        mats, block_ids = inputs
        gathered = vector[block_ids]
        product = jnp.einsum("cij,cjb->cib", mats, gathered, precision=lax.Precision.HIGHEST)
        running = running.at[block_ids.reshape(-1)].add(product.reshape(-1, vector.shape[1]))
        return running, None

    running, _ = lax.scan(one_block, jnp.zeros(vector.shape, jnp.float32), (matrices, node_ids))
    return running


def reference(waves, cell_matrix, connect, send_index, rotation):
    global_ids = assemble_ids(connect, send_index)
    previous = waves
    current = (operator_apply(waves, cell_matrix, global_ids) - centre * waves) / half_width
    for order in range(DEGREE - 1):
        image = operator_apply(current, cell_matrix, global_ids)
        following = 2.0 * (image - centre * current) / half_width - previous
        previous = current
        current = following
    return jnp.dot(current, rotation, precision=lax.Precision.HIGHEST, preferred_element_type=jnp.float32)
```

```python
import functools

import jax
import jax.numpy as jnp
from jax import lax
from jax.experimental import pallas as pl
from jax.experimental.pallas import tpu as pltpu
from jax.sharding import PartitionSpec as P

DEGREE = 8
LANES = 128


centre = 5.5
half_width = 9.5


def split(x):
    high = lax.reduce_precision(x, 8, 7)
    return high.astype(jnp.bfloat16), (x - high).astype(jnp.bfloat16)


def doubled(x, half):
    return x + pltpu.roll(x, half, 1)


def packed(x, half):
    high = x.astype(jnp.bfloat16)
    low = (x - high.astype(jnp.float32)).astype(jnp.bfloat16)
    lane = lax.broadcasted_iota(jnp.int32, x.shape, 1)
    return jnp.where(lane < half, high.astype(jnp.float32), low.astype(jnp.float32)).astype(
        jnp.bfloat16
    )


def mm(a, b):
    return jnp.dot(a, b, preferred_element_type=jnp.float32)


def filter_kernel(doms, owned, slots, half, high, low, pick, spread, start, out, pieces, ghosts, before, image):
    unroll = doms <= 8

    def over(body):
        if unroll:
            for d in range(doms):
                body(d)
        else:
            pl.loop(0, doms)(body)

    def begin(d):
        v = start[d]
        out[d] = v
        before[d] = jnp.zeros_like(v)
        pieces[d, :owned] = packed(v, half)

    over(begin)

    def one(step, _):
        def send(d):
            after = lax.rem(d + 1, doms) if not unroll else (d + 1) % doms
            ahead = lax.rem(d + doms - 1, doms) if not unroll else (d - 1) % doms
            g = mm(pick[d], pieces[d, :owned]).astype(jnp.bfloat16)
            pieces[after, owned : owned + slots] = g[:slots]
            pieces[ahead, owned + slots :] = g[slots:]

        over(send)

        def apply(d):
            x = pieces[d]
            y = mm(high[d], x) + mm(low[d], x)
            y = doubled(y, half)
            image[d] = y[:owned]
            after = lax.rem(d + 1, doms) if not unroll else (d + 1) % doms
            ahead = lax.rem(d + doms - 1, doms) if not unroll else (d - 1) % doms
            r = packed(y[owned:], half)
            ghosts[ahead, :slots] = r[:slots]
            ghosts[after, slots:] = r[slots:]

        over(apply)
        scale = jnp.where(step == 0, 1.0, 2.0)

        def update(d):
            y = image[d] + doubled(mm(spread[d], ghosts[d]), half)
            v = scale * y - before[d]
            before[d] = out[d]
            out[d] = v
            pieces[d, :owned] = packed(v, half)

        over(update)
        return 0

    lax.fori_loop(0, DEGREE, one, 0)


def shards(waves, cell_matrix, connect, send_index, rotation):
    owned = waves.shape[0]
    width = waves.shape[1]
    slots = send_index.shape[2]
    doms = lax.axis_size("dom")
    size = owned + 2 * slots
    seat = jax.nn.one_hot(connect, size, dtype=jnp.float32)
    half_way = jnp.einsum("cij,cjn->cin", cell_matrix, seat, precision=lax.Precision.HIGH)
    local = jnp.einsum("cim,cin->mn", seat, half_way, precision=lax.Precision.HIGH)
    node = jnp.arange(size)
    shift = jnp.where((node[:, None] == node[None, :]) & (node[:, None] < owned), centre, 0.0)
    local = (local - shift) / half_width
    row = jnp.zeros((8, size), jnp.float32).at[0, : 2 * slots].set(
        send_index.reshape(-1).astype(jnp.float32)
    )
    everyone = lax.all_gather(jnp.concatenate([local, row], axis=0), "dom")
    high, low = split(everyone[:, :size])
    index = everyone[:, size, : 2 * slots].astype(jnp.int32)
    pick = jax.nn.one_hot(index, owned, dtype=jnp.bfloat16)
    spread = jnp.swapaxes(pick, 1, 2)

    partial = jnp.dot(waves, rotation, precision=lax.Precision.HIGH, preferred_element_type=jnp.float32)
    turned = lax.psum_scatter(partial, "band", scatter_dimension=1, tiled=True)
    share = width // doms
    columns = lax.all_to_all(turned, "dom", split_axis=1, concat_axis=0, tiled=True)
    columns = columns.reshape(doms, owned, share)
    half = LANES // 2
    columns = jnp.pad(columns, ((0, 0), (0, 0), (0, half - share)))
    columns = jnp.concatenate([columns, columns], axis=2)
    vmem = pl.BlockSpec(memory_space=pltpu.VMEM)
    done = pl.pallas_call(
        functools.partial(filter_kernel, doms, owned, slots, half),
        out_shape=jax.ShapeDtypeStruct((doms, owned, LANES), jnp.float32),
        in_specs=[vmem] * 5,
        out_specs=vmem,
        scratch_shapes=[
            pltpu.VMEM((doms, size, LANES), jnp.bfloat16),
            pltpu.VMEM((doms, 2 * slots, LANES), jnp.bfloat16),
            pltpu.VMEM((doms, owned, LANES), jnp.float32),
            pltpu.VMEM((doms, owned, LANES), jnp.float32),
        ],
        compiler_params=pltpu.CompilerParams(vmem_limit_bytes=56 * 2**20),
        cost_estimate=pl.CostEstimate(
            flops=DEGREE * doms * 4 * size * size * LANES, bytes_accessed=2**24, transcendentals=0
        ),
    )(high, low, pick, spread, columns)
    back = done[:, :, :share].reshape(doms * owned, share)
    return lax.all_to_all(back, "dom", split_axis=0, concat_axis=1, tiled=True)


def solution(mesh):
    in_specs = (
        P("dom", "band"),
        P("dom", None, None),
        P("dom", None),
        P("dom", None, None),
        P("band", None),
    )
    out_specs = P("dom", "band")
    return jax.shard_map(shards, mesh=mesh, in_specs=in_specs, out_specs=out_specs, check_vma=False)
```

```python
import functools

import jax
import jax.numpy as jnp
from jax import lax
from jax.experimental import pallas as pl
from jax.experimental.pallas import tpu as pltpu
from jax.sharding import PartitionSpec as P

DEGREE = 8
LANES = 128
MESH = pl.DeviceIdType.MESH


centre = 5.5
half_width = 9.5


def split(x):
    high = lax.reduce_precision(x, 8, 7)
    return high.astype(jnp.bfloat16), (x - high).astype(jnp.bfloat16)


def doubled(x, half):
    return x + pltpu.roll(x, half, 1)


def packed(x, half):
    high = x.astype(jnp.bfloat16)
    low = (x - high.astype(jnp.float32)).astype(jnp.bfloat16)
    lane = lax.broadcasted_iota(jnp.int32, x.shape, 1)
    return jnp.where(lane < half, high.astype(jnp.float32), low.astype(jnp.float32)).astype(
        jnp.bfloat16
    )


def mm(a, b):
    return jnp.dot(a, b, preferred_element_type=jnp.float32)


def filter_kernel(doms, owned, slots, half, high, low, pick, spread, start, out, pieces, ghosts, before, image):
    unroll = doms <= 8

    def over(body):
        if unroll:
            for d in range(doms):
                body(d)
        else:
            pl.loop(0, doms)(body)

    def begin(d):
        v = start[d]
        out[d] = v
        before[d] = jnp.zeros_like(v)
        pieces[d, :owned] = packed(v, half)

    over(begin)

    def one(step, _):
        def send(d):
            after = lax.rem(d + 1, doms) if not unroll else (d + 1) % doms
            ahead = lax.rem(d + doms - 1, doms) if not unroll else (d - 1) % doms
            g = mm(pick[d], pieces[d, :owned]).astype(jnp.bfloat16)
            pieces[after, owned : owned + slots] = g[:slots]
            pieces[ahead, owned + slots :] = g[slots:]

        over(send)

        def apply(d):
            x = pieces[d]
            y = mm(high[d], x) + mm(low[d], x)
            y = doubled(y, half)
            image[d] = y[:owned]
            after = lax.rem(d + 1, doms) if not unroll else (d + 1) % doms
            ahead = lax.rem(d + doms - 1, doms) if not unroll else (d - 1) % doms
            r = packed(y[owned:], half)
            ghosts[ahead, :slots] = r[:slots]
            ghosts[after, slots:] = r[slots:]

        over(apply)
        scale = jnp.where(step == 0, 1.0, 2.0)

        def update(d):
            y = image[d] + doubled(mm(spread[d], ghosts[d]), half)
            v = scale * y - before[d]
            before[d] = out[d]
            out[d] = v
            pieces[d, :owned] = packed(v, half)

        over(update)
        return 0

    lax.fori_loop(0, DEGREE, one, 0)


def high_low(x):
    high = x.astype(jnp.bfloat16)
    return high, (x - high.astype(jnp.float32)).astype(jnp.bfloat16)


def fused_kernel(bands, owned, slots, waves, cells, conn, send, rotation, out, *scratch):
    (acc, from_left, from_right, everyone, matrix, pick, spread, sendbuf, colrecv, pieces, ghosts,
     state, before, image, sendback, backrecv,
     z_send, z_right, z_left, m_send, m_recv, a_send, a_recv, b_send, b_recv) = scratch
    doms = 8
    width = waves.shape[1]
    size = owned + 2 * slots
    half = LANES // 2
    rows = owned // 2
    me = lax.axis_index("dom")
    z = lax.axis_index("band")
    core = lax.rem(me, 2)
    place = lax.rem(lax.div(me, 2), 2)
    upper = lax.div(me, 4)
    sib = me + 1 - 2 * core
    x_next = me + 2 - 4 * place
    y_next = me + 4 - 8 * upper
    diag = x_next + 4 - 8 * upper

    barrier = pltpu.get_barrier_semaphore()
    for t in range(1, doms):
        pl.semaphore_signal(barrier, inc=1, device_id={"dom": lax.rem(me + t, doms)}, device_id_type=MESH)

    @pl.when(z > 0)
    def _():
        pl.semaphore_signal(barrier, inc=1, device_id={"band": z - 1}, device_id_type=MESH)

    @pl.when(z < bands - 1)
    def _():
        pl.semaphore_signal(barrier, inc=1, device_id={"band": z + 1}, device_id_type=MESH)

    beside = lax.div(z + bands - 1, bands) + lax.div(2 * bands - 2 - z, bands)
    pl.semaphore_wait(barrier, doms - 1 + beside)

    def to_right(j):
        return pltpu.make_async_remote_copy(
            src_ref=acc.at[j], dst_ref=from_left.at[j], send_sem=z_send.at[j],
            recv_sem=z_right.at[j], device_id={"band": z + 1}, device_id_type=MESH)

    def to_left(j):
        return pltpu.make_async_remote_copy(
            src_ref=acc.at[j], dst_ref=from_right.at[j], send_sem=z_send.at[j],
            recv_sem=z_left.at[j], device_id={"band": z - 1}, device_id_type=MESH)

    order = []
    for r in range(bands // 2):
        order += [bands - 1 - r, r]
    w_high, w_low = high_low(waves[...])
    for j in order:
        r_high, r_low = high_low(rotation[:, j * width : (j + 1) * width])
        acc[j] = mm(w_high, r_high) + (mm(w_high, r_low) + mm(w_low, r_high))
        if j > 0:
            @pl.when(z == 0)
            def _():
                to_right(j).start()
        if j < bands - 1:
            @pl.when(z == bands - 1)
            def _():
                to_left(j).start()

    node = lax.broadcasted_iota(jnp.int32, (size, conn.shape[1]), 0)
    total = jnp.zeros((size, size), jnp.float32)
    for c in range(cells.shape[0]):
        seat = jnp.where(node == conn[c : c + 1, :], 1.0, 0.0).astype(jnp.bfloat16)
        a_high, a_low = high_low(cells[c])
        b_high, b_low = high_low(mm(seat, a_high) + mm(seat, a_low))
        dims = (((1,), (1,)), ((), ()))
        total = total + (
            lax.dot_general(b_high, seat, dims, preferred_element_type=jnp.float32)
            + lax.dot_general(b_low, seat, dims, preferred_element_type=jnp.float32))
    r_at = lax.broadcasted_iota(jnp.int32, (size, size), 0)
    c_at = lax.broadcasted_iota(jnp.int32, (size, size), 1)
    shift = jnp.where((r_at == c_at) & (r_at < owned), centre, 0.0)
    everyone[me, :size] = (total - shift) / half_width
    everyone[me, size:] = jnp.zeros((8, size), jnp.float32)
    everyone[me, size : size + 2, :slots] = send[0].astype(jnp.float32)

    def pass_on(slot, to, k):
        return pltpu.make_async_remote_copy(
            src_ref=everyone.at[slot], dst_ref=everyone.at[slot], send_sem=m_send.at[k],
            recv_sem=m_recv.at[slot], device_id={"dom": to}, device_id_type=MESH)

    sent = [pass_on(me, x_next, 0), pass_on(me, y_next, 1), pass_on(me, sib, 2)]
    for copy in sent:
        copy.start()

    def relay_right(j, at):
        @pl.when(z == at)
        def _():
            to_right(j).wait_recv()
            acc[j] = acc[j] + from_left[j]
            to_right(j).start()

    def relay_left(j, at):
        @pl.when(z == at)
        def _():
            to_left(j).wait_recv()
            acc[j] = acc[j] + from_right[j]
            to_left(j).start()

    pass_on(x_next, sib, 0).wait_recv()
    pass_on(y_next, sib, 0).wait_recv()
    relays = [
        pass_on(x_next * (1 - core) + y_next * core, y_next * (1 - core) + x_next * core, 3),
        pass_on(x_next, sib, 4),
        pass_on(y_next, sib, 5),
    ]
    for copy in relays:
        copy.start()
    relay_right(3, 1)
    relay_left(0, 2)
    pass_on(diag, sib, 6).wait_recv()
    last = pass_on(diag, sib, 6)
    last.start()
    relay_left(0, 1)
    relay_right(3, 2)
    relay_right(2, 1)
    relay_left(1, 2)

    lane = lax.broadcasted_iota(jnp.int32, (rows, LANES), 1)
    low_lanes = lane < half

    def prepare(d):
        m_high, m_low = high_low(everyone[d, :size])
        matrix[d, :, :size] = m_high
        matrix[d, :, size:] = m_low
        tile = everyone[d, size:, :LANES]
        other = pltpu.roll(tile, half, 1)
        first_lanes = lax.broadcasted_iota(jnp.int32, (1, LANES), 1) < half
        row = jnp.where(first_lanes, tile[0:1], other[1:2]).astype(jnp.int32)
        at = lax.broadcasted_iota(jnp.int32, (owned, LANES), 0)
        hot = jnp.where(at == row, 1.0, 0.0)
        spread[d] = hot.astype(jnp.bfloat16)
        pick[d] = jnp.transpose(hot).astype(jnp.bfloat16)

    sib_slots = [sib, x_next + 1 - 2 * core, y_next + 1 - 2 * core, diag + 1 - 2 * core]
    for slot in sib_slots:
        pass_on(slot, sib, 6).wait_recv()
    for d in range(doms):
        prepare(d)

    finished = acc.at[z]
    for j in range(bands):
        if j > 0:
            @pl.when(z == j)
            def _():
                to_right(j).wait_recv()
                acc[j] = acc[j] + from_left[j]
        if j < bands - 1:
            @pl.when(z == j)
            def _():
                to_left(j).wait_recv()
                acc[j] = acc[j] + from_right[j]

    for p in range(doms // 2):
        top = finished[:rows, p * LANES : (p + 1) * LANES]
        bottom = finished[rows:, p * LANES : (p + 1) * LANES]
        sendbuf[2 * p] = jnp.where(low_lanes, top, pltpu.roll(bottom, half, 1))
        sendbuf[2 * p + 1] = jnp.where(low_lanes, pltpu.roll(top, half, 1), bottom)

    def exchange(t):
        to = lax.rem(me + t, doms)
        return pltpu.make_async_remote_copy(
            src_ref=sendbuf.at[to], dst_ref=colrecv.at[me], send_sem=a_send.at[t],
            recv_sem=a_recv.at[me], device_id={"dom": to}, device_id_type=MESH)

    def arrival(t):
        frm = lax.rem(me + t, doms)
        return pltpu.make_async_remote_copy(
            src_ref=sendbuf.at[frm], dst_ref=colrecv.at[frm], send_sem=a_send.at[t],
            recv_sem=a_recv.at[frm], device_id={"dom": frm}, device_id_type=MESH)

    for t in range(1, doms):
        exchange(t).start()
    colrecv[me] = sendbuf[me]
    for t in range(1, doms):
        arrival(t).wait_recv()

    def put(d, v):
        x = packed(v, half)
        pieces[d, :owned] = x
        pieces[d, size : size + owned] = x

    for d in range(doms):
        blk = colrecv[d]
        turned = pltpu.roll(blk, half, 1)
        v = jnp.concatenate(
            [jnp.where(low_lanes, blk, turned), jnp.where(low_lanes, turned, blk)], axis=0)
        state[d] = v
        before[d] = jnp.zeros_like(v)
        put(d, v)

    def spread_step():
        for d in range(doms):
            after, ahead = (d + 1) % doms, (d - 1) % doms
            g = mm(pick[d], pieces[d, :owned]).astype(jnp.bfloat16)
            for base in (0, size):
                pieces[after, base + owned : base + owned + slots] = g[:slots]
                pieces[ahead, base + owned + slots : base + size] = g[slots:]
        for d in range(doms):
            after, ahead = (d + 1) % doms, (d - 1) % doms
            y = doubled(mm(matrix[d], pieces[d]), half)
            image[d] = y[:owned]
            r = packed(y[owned:], half)
            ghosts[ahead, :slots] = r[:slots]
            ghosts[after, slots:] = r[slots:]

    def following(d, scale):
        y = image[d] + doubled(mm(spread[d], ghosts[d]), half)
        return scale * y - before[d]

    def one(step, _):
        spread_step()
        scale = jnp.where(step == 0, 1.0, 2.0)
        for d in range(doms):
            v = following(d, scale)
            before[d] = state[d]
            state[d] = v
            put(d, v)
        return 0

    lax.fori_loop(0, DEGREE - 1, one, 0)
    spread_step()

    def give(d):
        return pltpu.make_async_remote_copy(
            src_ref=sendback.at[d], dst_ref=backrecv.at[me], send_sem=b_send.at[d],
            recv_sem=b_recv.at[me], device_id={"dom": d}, device_id_type=MESH)

    for d in range(doms):
        v = following(d, 2.0)
        sendback[d] = jnp.where(low_lanes, v[:rows], v[rows:])

        @pl.when(me != d)
        def _():
            give(d).start()

    backrecv[me] = sendback[me]
    for d in range(doms):
        @pl.when(me != d)
        def _():
            pltpu.make_async_remote_copy(
                src_ref=sendback.at[d], dst_ref=backrecv.at[d], send_sem=b_send.at[d],
                recv_sem=b_recv.at[d], device_id={"dom": d}, device_id_type=MESH).wait_recv()

    for p in range(doms // 2):
        even, odd = backrecv[2 * p], backrecv[2 * p + 1]
        columns = slice(p * LANES, (p + 1) * LANES)
        out[:rows, columns] = jnp.where(low_lanes, even, pltpu.roll(odd, half, 1))
        out[rows:, columns] = jnp.where(low_lanes, pltpu.roll(even, half, 1), odd)

    for copy in sent + relays + [last]:
        copy.wait_send()
    for t in range(1, doms):
        exchange(t).wait_send()
    for d in range(doms):
        @pl.when(me != d)
        def _():
            give(d).wait_send()
    for j in range(bands):
        @pl.when(z < j)
        def _():
            to_right(j).wait_send()

        @pl.when(z > j)
        def _():
            to_left(j).wait_send()


def fused(waves, cell_matrix, connect, send_index, rotation):
    owned, width = waves.shape
    slots = send_index.shape[2]
    bands = lax.axis_size("band")
    size = owned + 2 * slots
    rows = owned // 2
    doms = 8
    vmem = pl.BlockSpec(memory_space=pltpu.VMEM)
    f32, b16 = jnp.float32, jnp.bfloat16
    dma = pltpu.SemaphoreType.DMA
    return pl.pallas_call(
        functools.partial(fused_kernel, bands, owned, slots),
        out_shape=jax.ShapeDtypeStruct((owned, width), f32),
        in_specs=[vmem] * 5,
        out_specs=vmem,
        scratch_shapes=[
            pltpu.VMEM((bands, owned, width), f32),
            pltpu.VMEM((bands, owned, width), f32),
            pltpu.VMEM((bands, owned, width), f32),
            pltpu.VMEM((doms, size + 8, size), f32),
            pltpu.VMEM((doms, size, 2 * size), b16),
            pltpu.VMEM((doms, 2 * slots, owned), b16),
            pltpu.VMEM((doms, owned, 2 * slots), b16),
            pltpu.VMEM((doms, rows, LANES), f32),
            pltpu.VMEM((doms, rows, LANES), f32),
            pltpu.VMEM((doms, 2 * size, LANES), b16),
            pltpu.VMEM((doms, 2 * slots, LANES), b16),
            pltpu.VMEM((doms, owned, LANES), f32),
            pltpu.VMEM((doms, owned, LANES), f32),
            pltpu.VMEM((doms, owned, LANES), f32),
            pltpu.VMEM((doms, rows, LANES), f32),
            pltpu.VMEM((doms, rows, LANES), f32),
            dma((bands,)), dma((bands,)), dma((bands,)),
            dma((7,)), dma((doms,)),
            dma((doms,)), dma((doms,)),
            dma((doms,)), dma((doms,)),
        ],
        compiler_params=pltpu.CompilerParams(
            vmem_limit_bytes=56 * 2**20, collective_id=0, has_side_effects=True),
        cost_estimate=pl.CostEstimate(
            flops=DEGREE * doms * 4 * size * size * LANES, bytes_accessed=2**24, transcendentals=0),
    )(waves, cell_matrix, connect, send_index, rotation)


def shards(waves, cell_matrix, connect, send_index, rotation):
    owned = waves.shape[0]
    width = waves.shape[1]
    slots = send_index.shape[2]
    doms = lax.axis_size("dom")
    if doms == 8 and width == doms * LANES // 2 and 2 * slots == LANES and lax.axis_size("band") == 4:
        return fused(waves, cell_matrix, connect, send_index, rotation)
    size = owned + 2 * slots
    seat = jax.nn.one_hot(connect, size, dtype=jnp.float32)
    half_way = jnp.einsum("cij,cjn->cin", cell_matrix, seat, precision=lax.Precision.HIGH)
    local = jnp.einsum("cim,cin->mn", seat, half_way, precision=lax.Precision.HIGH)
    node = jnp.arange(size)
    shift = jnp.where((node[:, None] == node[None, :]) & (node[:, None] < owned), centre, 0.0)
    local = (local - shift) / half_width
    row = jnp.zeros((8, size), jnp.float32).at[0, : 2 * slots].set(
        send_index.reshape(-1).astype(jnp.float32)
    )
    everyone = lax.all_gather(jnp.concatenate([local, row], axis=0), "dom")
    high, low = split(everyone[:, :size])
    index = everyone[:, size, : 2 * slots].astype(jnp.int32)
    pick = jax.nn.one_hot(index, owned, dtype=jnp.bfloat16)
    spread = jnp.swapaxes(pick, 1, 2)

    partial = jnp.dot(waves, rotation, precision=lax.Precision.HIGH, preferred_element_type=jnp.float32)
    turned = lax.psum_scatter(partial, "band", scatter_dimension=1, tiled=True)
    share = width // doms
    columns = lax.all_to_all(turned, "dom", split_axis=1, concat_axis=0, tiled=True)
    columns = columns.reshape(doms, owned, share)
    half = LANES // 2
    columns = jnp.pad(columns, ((0, 0), (0, 0), (0, half - share)))
    columns = jnp.concatenate([columns, columns], axis=2)
    vmem = pl.BlockSpec(memory_space=pltpu.VMEM)
    done = pl.pallas_call(
        functools.partial(filter_kernel, doms, owned, slots, half),
        out_shape=jax.ShapeDtypeStruct((doms, owned, LANES), jnp.float32),
        in_specs=[vmem] * 5,
        out_specs=vmem,
        scratch_shapes=[
            pltpu.VMEM((doms, size, LANES), jnp.bfloat16),
            pltpu.VMEM((doms, 2 * slots, LANES), jnp.bfloat16),
            pltpu.VMEM((doms, owned, LANES), jnp.float32),
            pltpu.VMEM((doms, owned, LANES), jnp.float32),
        ],
        compiler_params=pltpu.CompilerParams(vmem_limit_bytes=56 * 2**20),
        cost_estimate=pl.CostEstimate(
            flops=DEGREE * doms * 4 * size * size * LANES, bytes_accessed=2**24, transcendentals=0
        ),
    )(high, low, pick, spread, columns)
    back = done[:, :, :share].reshape(doms * owned, share)
    return lax.all_to_all(back, "dom", split_axis=0, concat_axis=1, tiled=True)


def solution(mesh):
    in_specs = (
        P("dom", "band"),
        P("dom", None, None),
        P("dom", None),
        P("dom", None, None),
        P("band", None),
    )
    out_specs = P("dom", "band")
    return jax.shard_map(shards, mesh=mesh, in_specs=in_specs, out_specs=out_specs, check_vma=False)
```

```python
import functools

import jax
import jax.numpy as jnp
from jax import lax
from jax.experimental import pallas as pl
from jax.experimental.pallas import tpu as pltpu
from jax.sharding import PartitionSpec as P

DEGREE = 8
LANES = 128
MESH = pl.DeviceIdType.MESH


centre = 5.5
half_width = 9.5


def split(x):
    high = lax.reduce_precision(x, 8, 7)
    return high.astype(jnp.bfloat16), (x - high).astype(jnp.bfloat16)


def doubled(x, half):
    return x + pltpu.roll(x, half, 1)


def packed(x, half):
    high = x.astype(jnp.bfloat16)
    low = (x - high.astype(jnp.float32)).astype(jnp.bfloat16)
    lane = lax.broadcasted_iota(jnp.int32, x.shape, 1)
    return jnp.where(lane < half, high.astype(jnp.float32), low.astype(jnp.float32)).astype(
        jnp.bfloat16
    )


def mm(a, b):
    return jnp.dot(a, b, preferred_element_type=jnp.float32)


def filter_kernel(doms, owned, slots, half, high, low, pick, spread, start, out, pieces, ghosts, before, image):
    unroll = doms <= 8

    def over(body):
        if unroll:
            for d in range(doms):
                body(d)
        else:
            pl.loop(0, doms)(body)

    def begin(d):
        v = start[d]
        out[d] = v
        before[d] = jnp.zeros_like(v)
        pieces[d, :owned] = packed(v, half)

    over(begin)

    def one(step, _):
        def send(d):
            after = lax.rem(d + 1, doms) if not unroll else (d + 1) % doms
            ahead = lax.rem(d + doms - 1, doms) if not unroll else (d - 1) % doms
            g = mm(pick[d], pieces[d, :owned]).astype(jnp.bfloat16)
            pieces[after, owned : owned + slots] = g[:slots]
            pieces[ahead, owned + slots :] = g[slots:]

        over(send)

        def apply(d):
            x = pieces[d]
            y = mm(high[d], x) + mm(low[d], x)
            y = doubled(y, half)
            image[d] = y[:owned]
            after = lax.rem(d + 1, doms) if not unroll else (d + 1) % doms
            ahead = lax.rem(d + doms - 1, doms) if not unroll else (d - 1) % doms
            r = packed(y[owned:], half)
            ghosts[ahead, :slots] = r[:slots]
            ghosts[after, slots:] = r[slots:]

        over(apply)
        scale = jnp.where(step == 0, 1.0, 2.0)

        def update(d):
            y = image[d] + doubled(mm(spread[d], ghosts[d]), half)
            v = scale * y - before[d]
            before[d] = out[d]
            out[d] = v
            pieces[d, :owned] = packed(v, half)

        over(update)
        return 0

    lax.fori_loop(0, DEGREE, one, 0)


def high_low(x):
    high = x.astype(jnp.bfloat16)
    return high, (x - high.astype(jnp.float32)).astype(jnp.bfloat16)


def fused_kernel(bands, owned, slots, waves, cells, conn, send, rotation, out, *scratch):
    (acc, from_left, from_right, everyone, matrix, pick, spread, sendbuf, colrecv, pieces, ghosts,
     state, before, image, sendback, backrecv,
     z_send, z_right, z_left, m_send, m_recv, a_send, a_recv, b_send, b_recv) = scratch
    doms = 8
    width = waves.shape[1]
    size = owned + 2 * slots
    half = LANES // 2
    rows = owned // 2
    me = lax.axis_index("dom")
    z = lax.axis_index("band")
    core = lax.rem(me, 2)
    place = lax.rem(lax.div(me, 2), 2)
    upper = lax.div(me, 4)
    sib = me + 1 - 2 * core
    x_next = me + 2 - 4 * place
    y_next = me + 4 - 8 * upper
    diag = x_next + 4 - 8 * upper

    barrier = pltpu.get_barrier_semaphore()
    for t in range(1, doms):
        pl.semaphore_signal(barrier, inc=1, device_id={"dom": lax.rem(me + t, doms)}, device_id_type=MESH)

    @pl.when(z > 0)
    def _():
        pl.semaphore_signal(barrier, inc=1, device_id={"band": z - 1}, device_id_type=MESH)

    @pl.when(z < bands - 1)
    def _():
        pl.semaphore_signal(barrier, inc=1, device_id={"band": z + 1}, device_id_type=MESH)

    beside = lax.div(z + bands - 1, bands) + lax.div(2 * bands - 2 - z, bands)
    pl.semaphore_wait(barrier, doms - 1 + beside)

    def part(h):
        return pl.ds(h * rows, rows)

    def to_right(j, h):
        return pltpu.make_async_remote_copy(
            src_ref=acc.at[j, part(h)], dst_ref=from_left.at[j, part(h)], send_sem=z_send.at[j, h],
            recv_sem=z_right.at[j, h], device_id={"band": z + 1}, device_id_type=MESH)

    def to_left(j, h):
        return pltpu.make_async_remote_copy(
            src_ref=acc.at[j, part(h)], dst_ref=from_right.at[j, part(h)], send_sem=z_send.at[j, h],
            recv_sem=z_left.at[j, h], device_id={"band": z - 1}, device_id_type=MESH)

    order = []
    for r in range(bands // 2):
        order += [bands - 1 - r, r]
    w_high, w_low = high_low(waves[...])
    for j in order:
        r_high, r_low = high_low(rotation[:, j * width : (j + 1) * width])
        acc[j] = mm(w_high, r_high) + (mm(w_high, r_low) + mm(w_low, r_high))
        if j > 0:
            @pl.when(z == 0)
            def _():
                for h in range(2):
                    to_right(j, h).start()
        if j < bands - 1:
            @pl.when(z == bands - 1)
            def _():
                for h in range(2):
                    to_left(j, h).start()

    node = lax.broadcasted_iota(jnp.int32, (size, conn.shape[1]), 0)
    total = jnp.zeros((size, size), jnp.float32)
    for c in range(cells.shape[1]):
        seat = jnp.where(node == conn[c : c + 1, :], 1.0, 0.0).astype(jnp.bfloat16)
        a_high, a_low = high_low(cells[:, c, :])
        b_high, b_low = high_low(mm(seat, a_high) + mm(seat, a_low))
        dims = (((1,), (1,)), ((), ()))
        total = total + (
            lax.dot_general(b_high, seat, dims, preferred_element_type=jnp.float32)
            + lax.dot_general(b_low, seat, dims, preferred_element_type=jnp.float32))
    r_at = lax.broadcasted_iota(jnp.int32, (size, size), 0)
    c_at = lax.broadcasted_iota(jnp.int32, (size, size), 1)
    shift = jnp.where((r_at == c_at) & (r_at < owned), centre, 0.0)
    everyone[me, :size] = (total - shift) / half_width
    everyone[me, size:] = jnp.zeros((8, size), jnp.float32)
    everyone[me, size : size + 2, :slots] = send[0].astype(jnp.float32)

    def pass_on(slot, to, k):
        return pltpu.make_async_remote_copy(
            src_ref=everyone.at[slot], dst_ref=everyone.at[slot], send_sem=m_send.at[k],
            recv_sem=m_recv.at[slot], device_id={"dom": to}, device_id_type=MESH)

    sent = [pass_on(me, x_next, 0), pass_on(me, y_next, 1), pass_on(me, sib, 2)]
    for copy in sent:
        copy.start()

    def relay_right(j, at, h):
        @pl.when(z == at)
        def _():
            to_right(j, h).wait_recv()
            acc[j, part(h)] = acc[j, part(h)] + from_left[j, part(h)]
            to_right(j, h).start()

    def relay_left(j, at, h):
        @pl.when(z == at)
        def _():
            to_left(j, h).wait_recv()
            acc[j, part(h)] = acc[j, part(h)] + from_right[j, part(h)]
            to_left(j, h).start()

    for h in range(2):
        relay_right(3, 1, h)
        relay_left(0, 2, h)
    pass_on(x_next, sib, 0).wait_recv()
    pass_on(y_next, sib, 0).wait_recv()
    relays = [
        pass_on(x_next * (1 - core) + y_next * core, y_next * (1 - core) + x_next * core, 3),
        pass_on(x_next, sib, 4),
        pass_on(y_next, sib, 5),
    ]
    for copy in relays:
        copy.start()
    for h in range(2):
        relay_left(0, 1, h)
        relay_right(3, 2, h)
        relay_right(2, 1, h)
        relay_left(1, 2, h)
    pass_on(diag, sib, 6).wait_recv()
    last = pass_on(diag, sib, 6)
    last.start()

    lane = lax.broadcasted_iota(jnp.int32, (rows, LANES), 1)
    low_lanes = lane < half

    def prepare(d):
        m_high, m_low = high_low(everyone[d, :size])
        matrix[d, :, :size] = m_high
        matrix[d, :, size:] = m_low
        tile = everyone[d, size:, :LANES]
        other = pltpu.roll(tile, half, 1)
        first_lanes = lax.broadcasted_iota(jnp.int32, (1, LANES), 1) < half
        row = jnp.where(first_lanes, tile[0:1], other[1:2]).astype(jnp.int32)
        at = lax.broadcasted_iota(jnp.int32, (owned, LANES), 0)
        hot = jnp.where(at == row, 1.0, 0.0)
        spread[d] = hot.astype(jnp.bfloat16)
        pick[d] = jnp.transpose(hot).astype(jnp.bfloat16)

    sib_slots = [sib, x_next + 1 - 2 * core, y_next + 1 - 2 * core, diag + 1 - 2 * core]
    for slot in sib_slots:
        pass_on(slot, sib, 6).wait_recv()
    for d in range(doms):
        prepare(d)

    quarter = rows // 2
    low_quarter = lax.broadcasted_iota(jnp.int32, (quarter, LANES), 1) < half

    def exchange(t, h):
        to = lax.rem(me + t, doms)
        share = pl.ds(h * quarter, quarter)
        return pltpu.make_async_remote_copy(
            src_ref=sendbuf.at[to, share], dst_ref=colrecv.at[me, share], send_sem=a_send.at[t, h],
            recv_sem=a_recv.at[me, h], device_id={"dom": to}, device_id_type=MESH)

    def arrival(t, h):
        frm = lax.rem(me + t, doms)
        share = pl.ds(h * quarter, quarter)
        return pltpu.make_async_remote_copy(
            src_ref=sendbuf.at[frm, share], dst_ref=colrecv.at[frm, share], send_sem=a_send.at[t, h],
            recv_sem=a_recv.at[frm, h], device_id={"dom": frm}, device_id_type=MESH)

    finished = acc.at[z]
    for h in range(2):
        for j in range(bands):
            if j > 0:
                @pl.when(z == j)
                def _():
                    to_right(j, h).wait_recv()
                    acc[j, part(h)] = acc[j, part(h)] + from_left[j, part(h)]
            if j < bands - 1:
                @pl.when(z == j)
                def _():
                    to_left(j, h).wait_recv()
                    acc[j, part(h)] = acc[j, part(h)] + from_right[j, part(h)]
        first, second = h * rows, h * rows + quarter
        to_rows = slice(h * quarter, (h + 1) * quarter)
        for p in range(doms // 2):
            columns = slice(p * LANES, (p + 1) * LANES)
            top = finished[first:second, columns]
            bottom = finished[second : second + quarter, columns]
            sendbuf[2 * p, to_rows] = jnp.where(low_quarter, top, pltpu.roll(bottom, half, 1))
            sendbuf[2 * p + 1, to_rows] = jnp.where(low_quarter, pltpu.roll(top, half, 1), bottom)
        for t in range(1, doms):
            exchange(t, h).start()
    colrecv[me] = sendbuf[me]
    for h in range(2):
        for t in range(1, doms):
            arrival(t, h).wait_recv()

    def put(d, v):
        x = packed(v, half)
        pieces[d, :owned] = x
        pieces[d, size : size + owned] = x

    for d in range(doms):
        blk = colrecv[d]
        turned = pltpu.roll(blk, half, 1)
        left, right = jnp.where(low_lanes, blk, turned), jnp.where(low_lanes, turned, blk)
        v = jnp.concatenate(
            [left[:quarter], right[:quarter], left[quarter:], right[quarter:]], axis=0)
        state[d] = v
        before[d] = jnp.zeros_like(v)
        put(d, v)

    def spread_step():
        for d in range(doms):
            after, ahead = (d + 1) % doms, (d - 1) % doms
            g = mm(pick[d], pieces[d, :owned]).astype(jnp.bfloat16)
            for base in (0, size):
                pieces[after, base + owned : base + owned + slots] = g[:slots]
                pieces[ahead, base + owned + slots : base + size] = g[slots:]
        for d in range(doms):
            after, ahead = (d + 1) % doms, (d - 1) % doms
            y = doubled(mm(matrix[d], pieces[d]), half)
            image[d] = y[:owned]
            r = packed(y[owned:], half)
            ghosts[ahead, :slots] = r[:slots]
            ghosts[after, slots:] = r[slots:]

    def following(d, scale):
        y = image[d] + doubled(mm(spread[d], ghosts[d]), half)
        return scale * y - before[d]

    def one(step, _):
        spread_step()
        scale = jnp.where(step == 0, 1.0, 2.0)
        for d in range(doms):
            v = following(d, scale)
            before[d] = state[d]
            state[d] = v
            put(d, v)
        return 0

    lax.fori_loop(0, DEGREE - 1, one, 0)
    spread_step()

    def give(d):
        return pltpu.make_async_remote_copy(
            src_ref=sendback.at[d], dst_ref=backrecv.at[me], send_sem=b_send.at[d],
            recv_sem=b_recv.at[me], device_id={"dom": d}, device_id_type=MESH)

    for d in range(doms):
        v = following(d, 2.0)
        sendback[d] = jnp.where(low_lanes, v[:rows], v[rows:])

        @pl.when(me != d)
        def _():
            give(d).start()

    backrecv[me] = sendback[me]
    for d in range(doms):
        @pl.when(me != d)
        def _():
            pltpu.make_async_remote_copy(
                src_ref=sendback.at[d], dst_ref=backrecv.at[d], send_sem=b_send.at[d],
                recv_sem=b_recv.at[d], device_id={"dom": d}, device_id_type=MESH).wait_recv()

    for p in range(doms // 2):
        even, odd = backrecv[2 * p], backrecv[2 * p + 1]
        columns = slice(p * LANES, (p + 1) * LANES)
        out[:rows, columns] = jnp.where(low_lanes, even, pltpu.roll(odd, half, 1))
        out[rows:, columns] = jnp.where(low_lanes, pltpu.roll(even, half, 1), odd)

    for copy in sent + relays + [last]:
        copy.wait_send()
    for t in range(1, doms):
        for h in range(2):
            exchange(t, h).wait_send()
    for d in range(doms):
        @pl.when(me != d)
        def _():
            give(d).wait_send()
    for j in range(bands):
        for h in range(2):
            @pl.when(z < j)
            def _():
                to_right(j, h).wait_send()

            @pl.when(z > j)
            def _():
                to_left(j, h).wait_send()


def fused(waves, cell_matrix, connect, send_index, rotation):
    owned, width = waves.shape
    slots = send_index.shape[2]
    bands = lax.axis_size("band")
    size = owned + 2 * slots
    rows = owned // 2
    doms = 8
    vmem = pl.BlockSpec(memory_space=pltpu.VMEM)
    f32, b16 = jnp.float32, jnp.bfloat16
    dma = pltpu.SemaphoreType.DMA
    return pl.pallas_call(
        functools.partial(fused_kernel, bands, owned, slots),
        out_shape=jax.ShapeDtypeStruct((owned, width), f32),
        in_specs=[vmem] * 5,
        out_specs=vmem,
        scratch_shapes=[
            pltpu.VMEM((bands, owned, width), f32),
            pltpu.VMEM((bands, owned, width), f32),
            pltpu.VMEM((bands, owned, width), f32),
            pltpu.VMEM((doms, size + 8, size), f32),
            pltpu.VMEM((doms, size, 2 * size), b16),
            pltpu.VMEM((doms, 2 * slots, owned), b16),
            pltpu.VMEM((doms, owned, 2 * slots), b16),
            pltpu.VMEM((doms, rows, LANES), f32),
            pltpu.VMEM((doms, rows, LANES), f32),
            pltpu.VMEM((doms, 2 * size, LANES), b16),
            pltpu.VMEM((doms, 2 * slots, LANES), b16),
            pltpu.VMEM((doms, owned, LANES), f32),
            pltpu.VMEM((doms, owned, LANES), f32),
            pltpu.VMEM((doms, owned, LANES), f32),
            pltpu.VMEM((doms, rows, LANES), f32),
            pltpu.VMEM((doms, rows, LANES), f32),
            dma((bands, 2)), dma((bands, 2)), dma((bands, 2)),
            dma((7,)), dma((doms,)),
            dma((doms, 2)), dma((doms, 2)),
            dma((doms,)), dma((doms,)),
        ],
        compiler_params=pltpu.CompilerParams(
            vmem_limit_bytes=56 * 2**20, collective_id=0, has_side_effects=True),
        cost_estimate=pl.CostEstimate(
            flops=DEGREE * doms * 4 * size * size * LANES, bytes_accessed=2**24, transcendentals=0),
    )(waves, jnp.swapaxes(cell_matrix, 0, 1), connect, send_index, rotation)


def shards(waves, cell_matrix, connect, send_index, rotation):
    owned = waves.shape[0]
    width = waves.shape[1]
    slots = send_index.shape[2]
    doms = lax.axis_size("dom")
    if doms == 8 and width == doms * LANES // 2 and 2 * slots == LANES and lax.axis_size("band") == 4:
        return fused(waves, cell_matrix, connect, send_index, rotation)
    size = owned + 2 * slots
    seat = jax.nn.one_hot(connect, size, dtype=jnp.float32)
    half_way = jnp.einsum("cij,cjn->cin", cell_matrix, seat, precision=lax.Precision.HIGH)
    local = jnp.einsum("cim,cin->mn", seat, half_way, precision=lax.Precision.HIGH)
    node = jnp.arange(size)
    shift = jnp.where((node[:, None] == node[None, :]) & (node[:, None] < owned), centre, 0.0)
    local = (local - shift) / half_width
    row = jnp.zeros((8, size), jnp.float32).at[0, : 2 * slots].set(
        send_index.reshape(-1).astype(jnp.float32)
    )
    everyone = lax.all_gather(jnp.concatenate([local, row], axis=0), "dom")
    high, low = split(everyone[:, :size])
    index = everyone[:, size, : 2 * slots].astype(jnp.int32)
    pick = jax.nn.one_hot(index, owned, dtype=jnp.bfloat16)
    spread = jnp.swapaxes(pick, 1, 2)

    partial = jnp.dot(waves, rotation, precision=lax.Precision.HIGH, preferred_element_type=jnp.float32)
    turned = lax.psum_scatter(partial, "band", scatter_dimension=1, tiled=True)
    share = width // doms
    columns = lax.all_to_all(turned, "dom", split_axis=1, concat_axis=0, tiled=True)
    columns = columns.reshape(doms, owned, share)
    half = LANES // 2
    columns = jnp.pad(columns, ((0, 0), (0, 0), (0, half - share)))
    columns = jnp.concatenate([columns, columns], axis=2)
    vmem = pl.BlockSpec(memory_space=pltpu.VMEM)
    done = pl.pallas_call(
        functools.partial(filter_kernel, doms, owned, slots, half),
        out_shape=jax.ShapeDtypeStruct((doms, owned, LANES), jnp.float32),
        in_specs=[vmem] * 5,
        out_specs=vmem,
        scratch_shapes=[
            pltpu.VMEM((doms, size, LANES), jnp.bfloat16),
            pltpu.VMEM((doms, 2 * slots, LANES), jnp.bfloat16),
            pltpu.VMEM((doms, owned, LANES), jnp.float32),
            pltpu.VMEM((doms, owned, LANES), jnp.float32),
        ],
        compiler_params=pltpu.CompilerParams(vmem_limit_bytes=56 * 2**20),
        cost_estimate=pl.CostEstimate(
            flops=DEGREE * doms * 4 * size * size * LANES, bytes_accessed=2**24, transcendentals=0
        ),
    )(high, low, pick, spread, columns)
    back = done[:, :, :share].reshape(doms * owned, share)
    return lax.all_to_all(back, "dom", split_axis=0, concat_axis=1, tiled=True)


def solution(mesh):
    in_specs = (
        P("dom", "band"),
        P("dom", None, None),
        P("dom", None),
        P("dom", None, None),
        P("band", None),
    )
    out_specs = P("dom", "band")
    return jax.shard_map(shards, mesh=mesh, in_specs=in_specs, out_specs=out_specs, check_vma=False)
```

```python
import functools

import jax
import jax.numpy as jnp
from jax import lax
from jax.experimental import pallas as pl
from jax.experimental.pallas import tpu as pltpu
from jax.sharding import PartitionSpec as P

DEGREE = 8
LANES = 128
MESH = pl.DeviceIdType.MESH
CUTS = 4


centre = 5.5
half_width = 9.5


def split(x):
    high = lax.reduce_precision(x, 8, 7)
    return high.astype(jnp.bfloat16), (x - high).astype(jnp.bfloat16)


def doubled(x, half):
    return x + pltpu.roll(x, half, 1)


def packed(x, half):
    high = x.astype(jnp.bfloat16)
    low = (x - high.astype(jnp.float32)).astype(jnp.bfloat16)
    lane = lax.broadcasted_iota(jnp.int32, x.shape, 1)
    return jnp.where(lane < half, high.astype(jnp.float32), low.astype(jnp.float32)).astype(
        jnp.bfloat16
    )


def mm(a, b):
    return jnp.dot(a, b, preferred_element_type=jnp.float32)


def filter_kernel(doms, owned, slots, half, high, low, pick, spread, start, out, pieces, ghosts, before, image):
    unroll = doms <= 8

    def over(body):
        if unroll:
            for d in range(doms):
                body(d)
        else:
            pl.loop(0, doms)(body)

    def begin(d):
        v = start[d]
        out[d] = v
        before[d] = jnp.zeros_like(v)
        pieces[d, :owned] = packed(v, half)

    over(begin)

    def one(step, _):
        def send(d):
            after = lax.rem(d + 1, doms) if not unroll else (d + 1) % doms
            ahead = lax.rem(d + doms - 1, doms) if not unroll else (d - 1) % doms
            g = mm(pick[d], pieces[d, :owned]).astype(jnp.bfloat16)
            pieces[after, owned : owned + slots] = g[:slots]
            pieces[ahead, owned + slots :] = g[slots:]

        over(send)

        def apply(d):
            x = pieces[d]
            y = mm(high[d], x) + mm(low[d], x)
            y = doubled(y, half)
            image[d] = y[:owned]
            after = lax.rem(d + 1, doms) if not unroll else (d + 1) % doms
            ahead = lax.rem(d + doms - 1, doms) if not unroll else (d - 1) % doms
            r = packed(y[owned:], half)
            ghosts[ahead, :slots] = r[:slots]
            ghosts[after, slots:] = r[slots:]

        over(apply)
        scale = jnp.where(step == 0, 1.0, 2.0)

        def update(d):
            y = image[d] + doubled(mm(spread[d], ghosts[d]), half)
            v = scale * y - before[d]
            before[d] = out[d]
            out[d] = v
            pieces[d, :owned] = packed(v, half)

        over(update)
        return 0

    lax.fori_loop(0, DEGREE, one, 0)


def high_low(x):
    high = x.astype(jnp.bfloat16)
    return high, (x - high.astype(jnp.float32)).astype(jnp.bfloat16)


def fused_kernel(bands, owned, slots, waves, cells, conn, send, rotation, out, *scratch):
    (acc, from_left, from_right, everyone, matrix, pick, spread, sendbuf, colrecv, pieces, ghosts,
     state, before, image, sendback, backrecv,
     z_send, z_right, z_left, m_send, m_recv, a_send, a_recv, b_send, b_recv) = scratch
    doms = 8
    width = waves.shape[1]
    size = owned + 2 * slots
    half = LANES // 2
    rows = owned // 2
    me = lax.axis_index("dom")
    z = lax.axis_index("band")
    core = lax.rem(me, 2)
    place = lax.rem(lax.div(me, 2), 2)
    upper = lax.div(me, 4)
    sib = me + 1 - 2 * core
    x_next = me + 2 - 4 * place
    y_next = me + 4 - 8 * upper
    diag = x_next + 4 - 8 * upper

    barrier = pltpu.get_barrier_semaphore()
    for t in range(1, doms):
        pl.semaphore_signal(barrier, inc=1, device_id={"dom": lax.rem(me + t, doms)}, device_id_type=MESH)

    @pl.when(z > 0)
    def _():
        pl.semaphore_signal(barrier, inc=1, device_id={"band": z - 1}, device_id_type=MESH)

    @pl.when(z < bands - 1)
    def _():
        pl.semaphore_signal(barrier, inc=1, device_id={"band": z + 1}, device_id_type=MESH)

    beside = lax.div(z + bands - 1, bands) + lax.div(2 * bands - 2 - z, bands)
    pl.semaphore_wait(barrier, doms - 1 + beside)

    cut = owned // CUTS

    def part(h):
        return pl.ds(h * cut, cut)

    def to_right(j, h):
        return pltpu.make_async_remote_copy(
            src_ref=acc.at[j, part(h)], dst_ref=from_left.at[j, part(h)], send_sem=z_send.at[j, h],
            recv_sem=z_right.at[j, h], device_id={"band": z + 1}, device_id_type=MESH)

    def to_left(j, h):
        return pltpu.make_async_remote_copy(
            src_ref=acc.at[j, part(h)], dst_ref=from_right.at[j, part(h)], send_sem=z_send.at[j, h],
            recv_sem=z_left.at[j, h], device_id={"band": z - 1}, device_id_type=MESH)

    order = []
    for r in range(bands // 2):
        order += [bands - 1 - r, r]
    w_high, w_low = high_low(waves[...])
    for j in order:
        r_high, r_low = high_low(rotation[:, j * width : (j + 1) * width])
        acc[j] = mm(w_high, r_high) + (mm(w_high, r_low) + mm(w_low, r_high))
        if j > 0:
            @pl.when(z == 0)
            def _():
                for h in range(CUTS):
                    to_right(j, h).start()
        if j < bands - 1:
            @pl.when(z == bands - 1)
            def _():
                for h in range(CUTS):
                    to_left(j, h).start()

    node = lax.broadcasted_iota(jnp.int32, (size, conn.shape[1]), 0)
    total = jnp.zeros((size, size), jnp.float32)
    for c in range(cells.shape[1]):
        seat = jnp.where(node == conn[c : c + 1, :], 1.0, 0.0).astype(jnp.bfloat16)
        a_high, a_low = high_low(cells[:, c, :])
        b_high, b_low = high_low(mm(seat, a_high) + mm(seat, a_low))
        dims = (((1,), (1,)), ((), ()))
        total = total + (
            lax.dot_general(b_high, seat, dims, preferred_element_type=jnp.float32)
            + lax.dot_general(b_low, seat, dims, preferred_element_type=jnp.float32))
    r_at = lax.broadcasted_iota(jnp.int32, (size, size), 0)
    c_at = lax.broadcasted_iota(jnp.int32, (size, size), 1)
    shift = jnp.where((r_at == c_at) & (r_at < owned), centre, 0.0)
    everyone[me, :size] = (total - shift) / half_width
    everyone[me, size:] = jnp.zeros((8, size), jnp.float32)
    everyone[me, size : size + 2, :slots] = send[0].astype(jnp.float32)

    def pass_on(slot, to, k):
        return pltpu.make_async_remote_copy(
            src_ref=everyone.at[slot], dst_ref=everyone.at[slot], send_sem=m_send.at[k],
            recv_sem=m_recv.at[slot], device_id={"dom": to}, device_id_type=MESH)

    sent = [pass_on(me, x_next, 0), pass_on(me, y_next, 1), pass_on(me, sib, 2)]
    for copy in sent:
        copy.start()

    def relay_right(j, at, h):
        @pl.when(z == at)
        def _():
            to_right(j, h).wait_recv()
            acc[j, part(h)] = acc[j, part(h)] + from_left[j, part(h)]
            to_right(j, h).start()

    def relay_left(j, at, h):
        @pl.when(z == at)
        def _():
            to_left(j, h).wait_recv()
            acc[j, part(h)] = acc[j, part(h)] + from_right[j, part(h)]
            to_left(j, h).start()

    for h in range(CUTS):
        relay_right(3, 1, h)
        relay_left(0, 2, h)
    pass_on(x_next, sib, 0).wait_recv()
    pass_on(y_next, sib, 0).wait_recv()
    relays = [
        pass_on(x_next * (1 - core) + y_next * core, y_next * (1 - core) + x_next * core, 3),
        pass_on(x_next, sib, 4),
        pass_on(y_next, sib, 5),
    ]
    for copy in relays:
        copy.start()
    for h in range(CUTS):
        relay_left(0, 1, h)
        relay_right(3, 2, h)
        relay_right(2, 1, h)
        relay_left(1, 2, h)
    pass_on(diag, sib, 6).wait_recv()
    last = pass_on(diag, sib, 6)
    last.start()

    lane = lax.broadcasted_iota(jnp.int32, (rows, LANES), 1)
    low_lanes = lane < half

    def prepare(d):
        m_high, m_low = high_low(everyone[d, :size])
        matrix[d, :, :size] = m_high
        matrix[d, :, size:] = m_low
        tile = everyone[d, size:, :LANES]
        other = pltpu.roll(tile, half, 1)
        first_lanes = lax.broadcasted_iota(jnp.int32, (1, LANES), 1) < half
        row = jnp.where(first_lanes, tile[0:1], other[1:2]).astype(jnp.int32)
        at = lax.broadcasted_iota(jnp.int32, (owned, LANES), 0)
        hot = jnp.where(at == row, 1.0, 0.0)
        spread[d] = hot.astype(jnp.bfloat16)
        pick[d] = jnp.transpose(hot).astype(jnp.bfloat16)

    sib_slots = [sib, x_next + 1 - 2 * core, y_next + 1 - 2 * core, diag + 1 - 2 * core]
    for slot in sib_slots:
        pass_on(slot, sib, 6).wait_recv()
    for d in range(doms):
        prepare(d)

    quarter = cut // 2
    low_quarter = lax.broadcasted_iota(jnp.int32, (quarter, LANES), 1) < half

    def exchange(t, h):
        to = lax.rem(me + t, doms)
        share = pl.ds(h * quarter, quarter)
        return pltpu.make_async_remote_copy(
            src_ref=sendbuf.at[to, share], dst_ref=colrecv.at[me, share], send_sem=a_send.at[t, h],
            recv_sem=a_recv.at[me, h], device_id={"dom": to}, device_id_type=MESH)

    def arrival(t, h):
        frm = lax.rem(me + t, doms)
        share = pl.ds(h * quarter, quarter)
        return pltpu.make_async_remote_copy(
            src_ref=sendbuf.at[frm, share], dst_ref=colrecv.at[frm, share], send_sem=a_send.at[t, h],
            recv_sem=a_recv.at[frm, h], device_id={"dom": frm}, device_id_type=MESH)

    finished = acc.at[z]
    for h in range(CUTS):
        for j in range(bands):
            if j > 0:
                @pl.when(z == j)
                def _():
                    to_right(j, h).wait_recv()
                    acc[j, part(h)] = acc[j, part(h)] + from_left[j, part(h)]
            if j < bands - 1:
                @pl.when(z == j)
                def _():
                    to_left(j, h).wait_recv()
                    acc[j, part(h)] = acc[j, part(h)] + from_right[j, part(h)]
        first, second = h * cut, h * cut + quarter
        to_rows = slice(h * quarter, (h + 1) * quarter)
        for p in range(doms // 2):
            columns = slice(p * LANES, (p + 1) * LANES)
            top = finished[first:second, columns]
            bottom = finished[second : second + quarter, columns]
            sendbuf[2 * p, to_rows] = jnp.where(low_quarter, top, pltpu.roll(bottom, half, 1))
            sendbuf[2 * p + 1, to_rows] = jnp.where(low_quarter, pltpu.roll(top, half, 1), bottom)
        for t in range(1, doms):
            exchange(t, h).start()
    colrecv[me] = sendbuf[me]
    for h in range(CUTS):
        for t in range(1, doms):
            arrival(t, h).wait_recv()

    def put(d, v):
        x = packed(v, half)
        pieces[d, :owned] = x
        pieces[d, size : size + owned] = x

    for d in range(doms):
        blk = colrecv[d]
        turned = pltpu.roll(blk, half, 1)
        left, right = jnp.where(low_lanes, blk, turned), jnp.where(low_lanes, turned, blk)
        sides = []
        for h in range(CUTS):
            at = slice(h * quarter, (h + 1) * quarter)
            sides += [left[at], right[at]]
        v = jnp.concatenate(sides, axis=0)
        state[d] = v
        before[d] = jnp.zeros_like(v)
        put(d, v)

    def spread_step():
        for d in range(doms):
            after, ahead = (d + 1) % doms, (d - 1) % doms
            g = mm(pick[d], pieces[d, :owned]).astype(jnp.bfloat16)
            for base in (0, size):
                pieces[after, base + owned : base + owned + slots] = g[:slots]
                pieces[ahead, base + owned + slots : base + size] = g[slots:]
        for d in range(doms):
            after, ahead = (d + 1) % doms, (d - 1) % doms
            y = doubled(mm(matrix[d], pieces[d]), half)
            image[d] = y[:owned]
            r = packed(y[owned:], half)
            ghosts[ahead, :slots] = r[:slots]
            ghosts[after, slots:] = r[slots:]

    def following(d, scale):
        y = image[d] + doubled(mm(spread[d], ghosts[d]), half)
        return scale * y - before[d]

    def one(step, _):
        spread_step()
        scale = jnp.where(step == 0, 1.0, 2.0)
        for d in range(doms):
            v = following(d, scale)
            before[d] = state[d]
            state[d] = v
            put(d, v)
        return 0

    lax.fori_loop(0, DEGREE - 1, one, 0)
    spread_step()

    def give(d):
        return pltpu.make_async_remote_copy(
            src_ref=sendback.at[d], dst_ref=backrecv.at[me], send_sem=b_send.at[d],
            recv_sem=b_recv.at[me], device_id={"dom": d}, device_id_type=MESH)

    for d in range(doms):
        v = following(d, 2.0)
        sendback[d] = jnp.where(low_lanes, v[:rows], v[rows:])

        @pl.when(me != d)
        def _():
            give(d).start()

    backrecv[me] = sendback[me]
    for d in range(doms):
        @pl.when(me != d)
        def _():
            pltpu.make_async_remote_copy(
                src_ref=sendback.at[d], dst_ref=backrecv.at[d], send_sem=b_send.at[d],
                recv_sem=b_recv.at[d], device_id={"dom": d}, device_id_type=MESH).wait_recv()

    for p in range(doms // 2):
        even, odd = backrecv[2 * p], backrecv[2 * p + 1]
        columns = slice(p * LANES, (p + 1) * LANES)
        out[:rows, columns] = jnp.where(low_lanes, even, pltpu.roll(odd, half, 1))
        out[rows:, columns] = jnp.where(low_lanes, pltpu.roll(even, half, 1), odd)

    for copy in sent + relays + [last]:
        copy.wait_send()
    for t in range(1, doms):
        for h in range(CUTS):
            exchange(t, h).wait_send()
    for d in range(doms):
        @pl.when(me != d)
        def _():
            give(d).wait_send()
    for j in range(bands):
        for h in range(CUTS):
            @pl.when(z < j)
            def _():
                to_right(j, h).wait_send()

            @pl.when(z > j)
            def _():
                to_left(j, h).wait_send()


def fused(waves, cell_matrix, connect, send_index, rotation):
    owned, width = waves.shape
    slots = send_index.shape[2]
    bands = lax.axis_size("band")
    size = owned + 2 * slots
    rows = owned // 2
    doms = 8
    vmem = pl.BlockSpec(memory_space=pltpu.VMEM)
    f32, b16 = jnp.float32, jnp.bfloat16
    dma = pltpu.SemaphoreType.DMA
    return pl.pallas_call(
        functools.partial(fused_kernel, bands, owned, slots),
        out_shape=jax.ShapeDtypeStruct((owned, width), f32),
        in_specs=[vmem] * 5,
        out_specs=vmem,
        scratch_shapes=[
            pltpu.VMEM((bands, owned, width), f32),
            pltpu.VMEM((bands, owned, width), f32),
            pltpu.VMEM((bands, owned, width), f32),
            pltpu.VMEM((doms, size + 8, size), f32),
            pltpu.VMEM((doms, size, 2 * size), b16),
            pltpu.VMEM((doms, 2 * slots, owned), b16),
            pltpu.VMEM((doms, owned, 2 * slots), b16),
            pltpu.VMEM((doms, rows, LANES), f32),
            pltpu.VMEM((doms, rows, LANES), f32),
            pltpu.VMEM((doms, 2 * size, LANES), b16),
            pltpu.VMEM((doms, 2 * slots, LANES), b16),
            pltpu.VMEM((doms, owned, LANES), f32),
            pltpu.VMEM((doms, owned, LANES), f32),
            pltpu.VMEM((doms, owned, LANES), f32),
            pltpu.VMEM((doms, rows, LANES), f32),
            pltpu.VMEM((doms, rows, LANES), f32),
            dma((bands, CUTS)), dma((bands, CUTS)), dma((bands, CUTS)),
            dma((7,)), dma((doms,)),
            dma((doms, CUTS)), dma((doms, CUTS)),
            dma((doms,)), dma((doms,)),
        ],
        compiler_params=pltpu.CompilerParams(
            vmem_limit_bytes=56 * 2**20, collective_id=0, has_side_effects=True),
        cost_estimate=pl.CostEstimate(
            flops=DEGREE * doms * 4 * size * size * LANES, bytes_accessed=2**24, transcendentals=0),
    )(waves, jnp.swapaxes(cell_matrix, 0, 1), connect, send_index, rotation)


def shards(waves, cell_matrix, connect, send_index, rotation):
    owned = waves.shape[0]
    width = waves.shape[1]
    slots = send_index.shape[2]
    doms = lax.axis_size("dom")
    if doms == 8 and width == doms * LANES // 2 and 2 * slots == LANES and lax.axis_size("band") == 4:
        return fused(waves, cell_matrix, connect, send_index, rotation)
    size = owned + 2 * slots
    seat = jax.nn.one_hot(connect, size, dtype=jnp.float32)
    half_way = jnp.einsum("cij,cjn->cin", cell_matrix, seat, precision=lax.Precision.HIGH)
    local = jnp.einsum("cim,cin->mn", seat, half_way, precision=lax.Precision.HIGH)
    node = jnp.arange(size)
    shift = jnp.where((node[:, None] == node[None, :]) & (node[:, None] < owned), centre, 0.0)
    local = (local - shift) / half_width
    row = jnp.zeros((8, size), jnp.float32).at[0, : 2 * slots].set(
        send_index.reshape(-1).astype(jnp.float32)
    )
    everyone = lax.all_gather(jnp.concatenate([local, row], axis=0), "dom")
    high, low = split(everyone[:, :size])
    index = everyone[:, size, : 2 * slots].astype(jnp.int32)
    pick = jax.nn.one_hot(index, owned, dtype=jnp.bfloat16)
    spread = jnp.swapaxes(pick, 1, 2)

    partial = jnp.dot(waves, rotation, precision=lax.Precision.HIGH, preferred_element_type=jnp.float32)
    turned = lax.psum_scatter(partial, "band", scatter_dimension=1, tiled=True)
    share = width // doms
    columns = lax.all_to_all(turned, "dom", split_axis=1, concat_axis=0, tiled=True)
    columns = columns.reshape(doms, owned, share)
    half = LANES // 2
    columns = jnp.pad(columns, ((0, 0), (0, 0), (0, half - share)))
    columns = jnp.concatenate([columns, columns], axis=2)
    vmem = pl.BlockSpec(memory_space=pltpu.VMEM)
    done = pl.pallas_call(
        functools.partial(filter_kernel, doms, owned, slots, half),
        out_shape=jax.ShapeDtypeStruct((doms, owned, LANES), jnp.float32),
        in_specs=[vmem] * 5,
        out_specs=vmem,
        scratch_shapes=[
            pltpu.VMEM((doms, size, LANES), jnp.bfloat16),
            pltpu.VMEM((doms, 2 * slots, LANES), jnp.bfloat16),
            pltpu.VMEM((doms, owned, LANES), jnp.float32),
            pltpu.VMEM((doms, owned, LANES), jnp.float32),
        ],
        compiler_params=pltpu.CompilerParams(vmem_limit_bytes=56 * 2**20),
        cost_estimate=pl.CostEstimate(
            flops=DEGREE * doms * 4 * size * size * LANES, bytes_accessed=2**24, transcendentals=0
        ),
    )(high, low, pick, spread, columns)
    back = done[:, :, :share].reshape(doms * owned, share)
    return lax.all_to_all(back, "dom", split_axis=0, concat_axis=1, tiled=True)


def solution(mesh):
    in_specs = (
        P("dom", "band"),
        P("dom", None, None),
        P("dom", None),
        P("dom", None, None),
        P("band", None),
    )
    out_specs = P("dom", "band")
    return jax.shard_map(shards, mesh=mesh, in_specs=in_specs, out_specs=out_specs, check_vma=False)
```

```python
import functools

import jax
import jax.numpy as jnp
from jax import lax
from jax.experimental import pallas as pl
from jax.experimental.pallas import tpu as pltpu
from jax.sharding import PartitionSpec as P

DEGREE = 8
LANES = 128
MESH = pl.DeviceIdType.MESH
CUTS = 4


centre = 5.5
half_width = 9.5


def split(x):
    high = lax.reduce_precision(x, 8, 7)
    return high.astype(jnp.bfloat16), (x - high).astype(jnp.bfloat16)


def doubled(x, half):
    return x + pltpu.roll(x, half, 1)


def packed(x, half):
    high = x.astype(jnp.bfloat16)
    low = (x - high.astype(jnp.float32)).astype(jnp.bfloat16)
    lane = lax.broadcasted_iota(jnp.int32, x.shape, 1)
    return jnp.where(lane < half, high.astype(jnp.float32), low.astype(jnp.float32)).astype(
        jnp.bfloat16
    )


def mm(a, b):
    return jnp.dot(a, b, preferred_element_type=jnp.float32)


def filter_kernel(doms, owned, slots, half, high, low, pick, spread, start, out, pieces, ghosts, before, image):
    unroll = doms <= 8

    def over(body):
        if unroll:
            for d in range(doms):
                body(d)
        else:
            pl.loop(0, doms)(body)

    def begin(d):
        v = start[d]
        out[d] = v
        before[d] = jnp.zeros_like(v)
        pieces[d, :owned] = packed(v, half)

    over(begin)

    def one(step, _):
        def send(d):
            after = lax.rem(d + 1, doms) if not unroll else (d + 1) % doms
            ahead = lax.rem(d + doms - 1, doms) if not unroll else (d - 1) % doms
            g = mm(pick[d], pieces[d, :owned]).astype(jnp.bfloat16)
            pieces[after, owned : owned + slots] = g[:slots]
            pieces[ahead, owned + slots :] = g[slots:]

        over(send)

        def apply(d):
            x = pieces[d]
            y = mm(high[d], x) + mm(low[d], x)
            y = doubled(y, half)
            image[d] = y[:owned]
            after = lax.rem(d + 1, doms) if not unroll else (d + 1) % doms
            ahead = lax.rem(d + doms - 1, doms) if not unroll else (d - 1) % doms
            r = packed(y[owned:], half)
            ghosts[ahead, :slots] = r[:slots]
            ghosts[after, slots:] = r[slots:]

        over(apply)
        scale = jnp.where(step == 0, 1.0, 2.0)

        def update(d):
            y = image[d] + doubled(mm(spread[d], ghosts[d]), half)
            v = scale * y - before[d]
            before[d] = out[d]
            out[d] = v
            pieces[d, :owned] = packed(v, half)

        over(update)
        return 0

    lax.fori_loop(0, DEGREE, one, 0)


def high_low(x):
    high = x.astype(jnp.bfloat16)
    return high, (x - high.astype(jnp.float32)).astype(jnp.bfloat16)


def fused_kernel(bands, owned, slots, waves, cells, conn, send, rotation, out, *scratch):
    (acc, from_left, from_right, everyone, matrix, pick, spread, sendbuf, colrecv, pieces, ghosts,
     state, before, image, sendback, backrecv,
     z_send, z_right, z_left, m_send, m_recv, a_send, a_recv, b_send, b_recv) = scratch
    doms = 8
    width = waves.shape[1]
    size = owned + 2 * slots
    half = LANES // 2
    rows = owned // 2
    me = lax.axis_index("dom")
    z = lax.axis_index("band")
    core = lax.rem(me, 2)
    place = lax.rem(lax.div(me, 2), 2)
    upper = lax.div(me, 4)
    sib = me + 1 - 2 * core
    x_next = me + 2 - 4 * place
    y_next = me + 4 - 8 * upper
    diag = x_next + 4 - 8 * upper

    barrier = pltpu.get_barrier_semaphore()
    for t in range(1, doms):
        pl.semaphore_signal(barrier, inc=1, device_id={"dom": lax.rem(me + t, doms)}, device_id_type=MESH)

    @pl.when(z > 0)
    def _():
        pl.semaphore_signal(barrier, inc=1, device_id={"band": z - 1}, device_id_type=MESH)

    @pl.when(z < bands - 1)
    def _():
        pl.semaphore_signal(barrier, inc=1, device_id={"band": z + 1}, device_id_type=MESH)

    beside = lax.div(z + bands - 1, bands) + lax.div(2 * bands - 2 - z, bands)
    pl.semaphore_wait(barrier, doms - 1 + beside)

    cut = owned // CUTS

    def part(h):
        return pl.ds(h * cut, cut)

    def to_right(j, h):
        return pltpu.make_async_remote_copy(
            src_ref=acc.at[j, part(h)], dst_ref=from_left.at[j, part(h)], send_sem=z_send.at[j, h],
            recv_sem=z_right.at[j, h], device_id={"band": z + 1}, device_id_type=MESH)

    def to_left(j, h):
        return pltpu.make_async_remote_copy(
            src_ref=acc.at[j, part(h)], dst_ref=from_right.at[j, part(h)], send_sem=z_send.at[j, h],
            recv_sem=z_left.at[j, h], device_id={"band": z - 1}, device_id_type=MESH)

    order = []
    for r in range(bands // 2):
        order += [bands - 1 - r, r]
    w_high, w_low = high_low(waves[...])
    for j in order:
        r_high, r_low = high_low(rotation[:, j * width : (j + 1) * width])
        acc[j] = mm(w_high, r_high) + (mm(w_high, r_low) + mm(w_low, r_high))
        if j > 0:
            @pl.when(z == 0)
            def _():
                for h in range(CUTS):
                    to_right(j, h).start()
        if j < bands - 1:
            @pl.when(z == bands - 1)
            def _():
                for h in range(CUTS):
                    to_left(j, h).start()

    node = lax.broadcasted_iota(jnp.int32, (size, conn.shape[1]), 0)
    total = jnp.zeros((size, size), jnp.float32)
    for c in range(cells.shape[1]):
        seat = jnp.where(node == conn[c : c + 1, :], 1.0, 0.0).astype(jnp.bfloat16)
        a_high, a_low = high_low(cells[:, c, :])
        b_high, b_low = high_low(mm(seat, a_high) + mm(seat, a_low))
        dims = (((1,), (1,)), ((), ()))
        total = total + (
            lax.dot_general(b_high, seat, dims, preferred_element_type=jnp.float32)
            + lax.dot_general(b_low, seat, dims, preferred_element_type=jnp.float32))
    r_at = lax.broadcasted_iota(jnp.int32, (size, size), 0)
    c_at = lax.broadcasted_iota(jnp.int32, (size, size), 1)
    shift = jnp.where((r_at == c_at) & (r_at < owned), centre, 0.0)
    total = (total - shift) / half_width
    everyone[me, :rows] = total[:rows]
    everyone[me, rows:owned, rows:] = total[rows:owned, rows:]
    everyone[me, rows:owned, :rows] = total[owned:, owned:]
    everyone[me, owned:] = jnp.zeros((8, size), jnp.float32)
    everyone[me, owned : owned + 2, :slots] = send[0].astype(jnp.float32)

    def pass_on(slot, to, k):
        return pltpu.make_async_remote_copy(
            src_ref=everyone.at[slot], dst_ref=everyone.at[slot], send_sem=m_send.at[k],
            recv_sem=m_recv.at[slot], device_id={"dom": to}, device_id_type=MESH)

    sent = [pass_on(me, x_next, 0), pass_on(me, y_next, 1), pass_on(me, sib, 2)]
    for copy in sent:
        copy.start()

    def relay_right(j, at, h):
        @pl.when(z == at)
        def _():
            to_right(j, h).wait_recv()
            acc[j, part(h)] = acc[j, part(h)] + from_left[j, part(h)]
            to_right(j, h).start()

    def relay_left(j, at, h):
        @pl.when(z == at)
        def _():
            to_left(j, h).wait_recv()
            acc[j, part(h)] = acc[j, part(h)] + from_right[j, part(h)]
            to_left(j, h).start()

    for h in range(CUTS):
        relay_right(3, 1, h)
        relay_left(0, 2, h)
    pass_on(x_next, sib, 0).wait_recv()
    pass_on(y_next, sib, 0).wait_recv()
    relays = [
        pass_on(x_next * (1 - core) + y_next * core, y_next * (1 - core) + x_next * core, 3),
        pass_on(x_next, sib, 4),
        pass_on(y_next, sib, 5),
    ]
    for copy in relays:
        copy.start()
    for h in range(CUTS):
        relay_left(0, 1, h)
        relay_right(3, 2, h)
        relay_right(2, 1, h)
        relay_left(1, 2, h)
    pass_on(diag, sib, 6).wait_recv()
    last = pass_on(diag, sib, 6)
    last.start()

    lane = lax.broadcasted_iota(jnp.int32, (rows, LANES), 1)
    low_lanes = lane < half

    def prepare(d):
        upper_rows = everyone[d, :rows]
        middle = everyone[d, rows:owned]
        whole = jnp.concatenate([
            upper_rows,
            jnp.concatenate([jnp.transpose(upper_rows[:, rows:owned]), middle[:, rows:]], axis=1),
            jnp.concatenate([
                jnp.transpose(upper_rows[:, owned:]), jnp.transpose(middle[:, owned:]),
                middle[:, :rows]], axis=1)], axis=0)
        m_high, m_low = high_low(whole)
        matrix[d, :, :size] = m_high
        matrix[d, :, size:] = m_low
        tile = everyone[d, owned:, :LANES]
        other = pltpu.roll(tile, half, 1)
        first_lanes = lax.broadcasted_iota(jnp.int32, (1, LANES), 1) < half
        row = jnp.where(first_lanes, tile[0:1], other[1:2]).astype(jnp.int32)
        at = lax.broadcasted_iota(jnp.int32, (owned, LANES), 0)
        hot = jnp.where(at == row, 1.0, 0.0)
        spread[d] = hot.astype(jnp.bfloat16)
        pick[d] = jnp.transpose(hot).astype(jnp.bfloat16)

    sib_slots = [sib, x_next + 1 - 2 * core, y_next + 1 - 2 * core, diag + 1 - 2 * core]
    for slot in sib_slots:
        pass_on(slot, sib, 6).wait_recv()
    for d in range(doms):
        prepare(d)

    quarter = cut // 2
    low_quarter = lax.broadcasted_iota(jnp.int32, (quarter, LANES), 1) < half

    def exchange(t, h):
        to = lax.rem(me + t, doms)
        share = pl.ds(h * quarter, quarter)
        return pltpu.make_async_remote_copy(
            src_ref=sendbuf.at[to, share], dst_ref=colrecv.at[me, share], send_sem=a_send.at[t, h],
            recv_sem=a_recv.at[me, h], device_id={"dom": to}, device_id_type=MESH)

    def arrival(t, h):
        frm = lax.rem(me + t, doms)
        share = pl.ds(h * quarter, quarter)
        return pltpu.make_async_remote_copy(
            src_ref=sendbuf.at[frm, share], dst_ref=colrecv.at[frm, share], send_sem=a_send.at[t, h],
            recv_sem=a_recv.at[frm, h], device_id={"dom": frm}, device_id_type=MESH)

    finished = acc.at[z]
    for h in range(CUTS):
        for j in range(bands):
            if j > 0:
                @pl.when(z == j)
                def _():
                    to_right(j, h).wait_recv()
                    acc[j, part(h)] = acc[j, part(h)] + from_left[j, part(h)]
            if j < bands - 1:
                @pl.when(z == j)
                def _():
                    to_left(j, h).wait_recv()
                    acc[j, part(h)] = acc[j, part(h)] + from_right[j, part(h)]
        first, second = h * cut, h * cut + quarter
        to_rows = slice(h * quarter, (h + 1) * quarter)
        for p in range(doms // 2):
            columns = slice(p * LANES, (p + 1) * LANES)
            top = finished[first:second, columns]
            bottom = finished[second : second + quarter, columns]
            sendbuf[2 * p, to_rows] = jnp.where(low_quarter, top, pltpu.roll(bottom, half, 1))
            sendbuf[2 * p + 1, to_rows] = jnp.where(low_quarter, pltpu.roll(top, half, 1), bottom)
        for t in range(1, doms):
            exchange(t, h).start()
    colrecv[me] = sendbuf[me]
    for h in range(CUTS):
        for t in range(1, doms):
            arrival(t, h).wait_recv()

    def put(d, v):
        x = packed(v, half)
        pieces[d, :owned] = x
        pieces[d, size : size + owned] = x

    for d in range(doms):
        blk = colrecv[d]
        turned = pltpu.roll(blk, half, 1)
        left, right = jnp.where(low_lanes, blk, turned), jnp.where(low_lanes, turned, blk)
        sides = []
        for h in range(CUTS):
            at = slice(h * quarter, (h + 1) * quarter)
            sides += [left[at], right[at]]
        v = jnp.concatenate(sides, axis=0)
        state[d] = v
        before[d] = jnp.zeros_like(v)
        put(d, v)

    def spread_step():
        for d in range(doms):
            after, ahead = (d + 1) % doms, (d - 1) % doms
            g = mm(pick[d], pieces[d, :owned]).astype(jnp.bfloat16)
            for base in (0, size):
                pieces[after, base + owned : base + owned + slots] = g[:slots]
                pieces[ahead, base + owned + slots : base + size] = g[slots:]
        for d in range(doms):
            after, ahead = (d + 1) % doms, (d - 1) % doms
            y = doubled(mm(matrix[d], pieces[d]), half)
            image[d] = y[:owned]
            r = packed(y[owned:], half)
            ghosts[ahead, :slots] = r[:slots]
            ghosts[after, slots:] = r[slots:]

    def following(d, scale):
        y = image[d] + doubled(mm(spread[d], ghosts[d]), half)
        return scale * y - before[d]

    def one(step, _):
        spread_step()
        scale = jnp.where(step == 0, 1.0, 2.0)
        for d in range(doms):
            v = following(d, scale)
            before[d] = state[d]
            state[d] = v
            put(d, v)
        return 0

    lax.fori_loop(0, DEGREE - 1, one, 0)
    spread_step()

    def give(d):
        return pltpu.make_async_remote_copy(
            src_ref=sendback.at[d], dst_ref=backrecv.at[me], send_sem=b_send.at[d],
            recv_sem=b_recv.at[me], device_id={"dom": d}, device_id_type=MESH)

    for d in range(doms):
        v = following(d, 2.0)
        sendback[d] = jnp.where(low_lanes, v[:rows], v[rows:])

        @pl.when(me != d)
        def _():
            give(d).start()

    backrecv[me] = sendback[me]
    for d in range(doms):
        @pl.when(me != d)
        def _():
            pltpu.make_async_remote_copy(
                src_ref=sendback.at[d], dst_ref=backrecv.at[d], send_sem=b_send.at[d],
                recv_sem=b_recv.at[d], device_id={"dom": d}, device_id_type=MESH).wait_recv()

    for p in range(doms // 2):
        even, odd = backrecv[2 * p], backrecv[2 * p + 1]
        columns = slice(p * LANES, (p + 1) * LANES)
        out[:rows, columns] = jnp.where(low_lanes, even, pltpu.roll(odd, half, 1))
        out[rows:, columns] = jnp.where(low_lanes, pltpu.roll(even, half, 1), odd)

    for copy in sent + relays + [last]:
        copy.wait_send()
    for t in range(1, doms):
        for h in range(CUTS):
            exchange(t, h).wait_send()
    for d in range(doms):
        @pl.when(me != d)
        def _():
            give(d).wait_send()
    for j in range(bands):
        for h in range(CUTS):
            @pl.when(z < j)
            def _():
                to_right(j, h).wait_send()

            @pl.when(z > j)
            def _():
                to_left(j, h).wait_send()


def fused(waves, cell_matrix, connect, send_index, rotation):
    owned, width = waves.shape
    slots = send_index.shape[2]
    bands = lax.axis_size("band")
    size = owned + 2 * slots
    rows = owned // 2
    doms = 8
    vmem = pl.BlockSpec(memory_space=pltpu.VMEM)
    f32, b16 = jnp.float32, jnp.bfloat16
    dma = pltpu.SemaphoreType.DMA
    return pl.pallas_call(
        functools.partial(fused_kernel, bands, owned, slots),
        out_shape=jax.ShapeDtypeStruct((owned, width), f32),
        in_specs=[vmem] * 5,
        out_specs=vmem,
        scratch_shapes=[
            pltpu.VMEM((bands, owned, width), f32),
            pltpu.VMEM((bands, owned, width), f32),
            pltpu.VMEM((bands, owned, width), f32),
            pltpu.VMEM((doms, owned + 8, size), f32),
            pltpu.VMEM((doms, size, 2 * size), b16),
            pltpu.VMEM((doms, 2 * slots, owned), b16),
            pltpu.VMEM((doms, owned, 2 * slots), b16),
            pltpu.VMEM((doms, rows, LANES), f32),
            pltpu.VMEM((doms, rows, LANES), f32),
            pltpu.VMEM((doms, 2 * size, LANES), b16),
            pltpu.VMEM((doms, 2 * slots, LANES), b16),
            pltpu.VMEM((doms, owned, LANES), f32),
            pltpu.VMEM((doms, owned, LANES), f32),
            pltpu.VMEM((doms, owned, LANES), f32),
            pltpu.VMEM((doms, rows, LANES), f32),
            pltpu.VMEM((doms, rows, LANES), f32),
            dma((bands, CUTS)), dma((bands, CUTS)), dma((bands, CUTS)),
            dma((7,)), dma((doms,)),
            dma((doms, CUTS)), dma((doms, CUTS)),
            dma((doms,)), dma((doms,)),
        ],
        compiler_params=pltpu.CompilerParams(
            vmem_limit_bytes=56 * 2**20, collective_id=0, has_side_effects=True),
        cost_estimate=pl.CostEstimate(
            flops=DEGREE * doms * 4 * size * size * LANES, bytes_accessed=2**24, transcendentals=0),
    )(waves, jnp.swapaxes(cell_matrix, 0, 1), connect, send_index, rotation)


def shards(waves, cell_matrix, connect, send_index, rotation):
    owned = waves.shape[0]
    width = waves.shape[1]
    slots = send_index.shape[2]
    doms = lax.axis_size("dom")
    if doms == 8 and width == doms * LANES // 2 and 2 * slots == LANES and owned == 2 * LANES and lax.axis_size("band") == 4:
        return fused(waves, cell_matrix, connect, send_index, rotation)
    size = owned + 2 * slots
    seat = jax.nn.one_hot(connect, size, dtype=jnp.float32)
    half_way = jnp.einsum("cij,cjn->cin", cell_matrix, seat, precision=lax.Precision.HIGH)
    local = jnp.einsum("cim,cin->mn", seat, half_way, precision=lax.Precision.HIGH)
    node = jnp.arange(size)
    shift = jnp.where((node[:, None] == node[None, :]) & (node[:, None] < owned), centre, 0.0)
    local = (local - shift) / half_width
    row = jnp.zeros((8, size), jnp.float32).at[0, : 2 * slots].set(
        send_index.reshape(-1).astype(jnp.float32)
    )
    everyone = lax.all_gather(jnp.concatenate([local, row], axis=0), "dom")
    high, low = split(everyone[:, :size])
    index = everyone[:, size, : 2 * slots].astype(jnp.int32)
    pick = jax.nn.one_hot(index, owned, dtype=jnp.bfloat16)
    spread = jnp.swapaxes(pick, 1, 2)

    partial = jnp.dot(waves, rotation, precision=lax.Precision.HIGH, preferred_element_type=jnp.float32)
    turned = lax.psum_scatter(partial, "band", scatter_dimension=1, tiled=True)
    share = width // doms
    columns = lax.all_to_all(turned, "dom", split_axis=1, concat_axis=0, tiled=True)
    columns = columns.reshape(doms, owned, share)
    half = LANES // 2
    columns = jnp.pad(columns, ((0, 0), (0, 0), (0, half - share)))
    columns = jnp.concatenate([columns, columns], axis=2)
    vmem = pl.BlockSpec(memory_space=pltpu.VMEM)
    done = pl.pallas_call(
        functools.partial(filter_kernel, doms, owned, slots, half),
        out_shape=jax.ShapeDtypeStruct((doms, owned, LANES), jnp.float32),
        in_specs=[vmem] * 5,
        out_specs=vmem,
        scratch_shapes=[
            pltpu.VMEM((doms, size, LANES), jnp.bfloat16),
            pltpu.VMEM((doms, 2 * slots, LANES), jnp.bfloat16),
            pltpu.VMEM((doms, owned, LANES), jnp.float32),
            pltpu.VMEM((doms, owned, LANES), jnp.float32),
        ],
        compiler_params=pltpu.CompilerParams(vmem_limit_bytes=56 * 2**20),
        cost_estimate=pl.CostEstimate(
            flops=DEGREE * doms * 4 * size * size * LANES, bytes_accessed=2**24, transcendentals=0
        ),
    )(high, low, pick, spread, columns)
    back = done[:, :, :share].reshape(doms * owned, share)
    return lax.all_to_all(back, "dom", split_axis=0, concat_axis=1, tiled=True)


def solution(mesh):
    in_specs = (
        P("dom", "band"),
        P("dom", None, None),
        P("dom", None),
        P("dom", None, None),
        P("band", None),
    )
    out_specs = P("dom", "band")
    return jax.shard_map(shards, mesh=mesh, in_specs=in_specs, out_specs=out_specs, check_vma=False)
```
